512 devices in a mesh: event: 4 (over x_lo, core), tile: 128 (over y, z, x_hi).
Axes of the slice: x: 4 (x_hi: 2, x_lo: 2; x = x_hi * 2 + x_lo), y: 4, z: 16, core: 2. Of those that a mesh axis runs over, the one named last changes fastest.
Arguments:
- surf_depth: bfloat16 [4, 2048, 4096], P('event', 'tile'), may hold values from 0.019897461 to 0.19921875
- surf_mid: bfloat16 [4, 2048, 4096], P('event', 'tile'), may hold values from 0.019897461 to 0.19921875
- surf_seed: bfloat16 [4, 2048, 4096], P('event', 'tile'), may hold values from -6 to 6
- stream: int32 [2048, 4096], P('tile'), may hold values 0 or 1
- infil: float32 [256, 512], P('tile'), may hold values from 0.05 to 0.4
- diffus: float32 [256, 512], P('tile'), may hold values from 0.03 to 0.12
- leakance: float32 [512, 256], P('tile'), may hold values from 0.005 to 0.05
- active: int32 [512, 256], P('tile'), may hold values 0 or 1
- jacobi_coef: float32 [16, 512, 256], P(None, 'tile'), may hold values from 0.1 to 0.16
- head_seed: float32 [4, 16, 512, 256], P('event', None, 'tile'), may hold values from -6 to 6
- top_head: float32 [4, 512, 256], P('event', 'tile'), may hold values from -0.6 to 0.6
Outputs:
- depth_adj: bfloat16 [4, 2048, 4096], P('event', 'tile')
- head_adj: float32 [4, 16, 512, 256], P('event', None, 'tile')
- recharge_adj: float32 [4, 512, 256], P('event', 'tile')
- grad_w: float32 [256, 512], P('tile')
- grad_g: float32 [256, 512], P('tile')
- grad_lk: float32 [512, 256], P('tile')
The draws below stay inside these ranges and needn't reach their ends.
All inputs are finite; a program needn't handle non-finite values. No bound on the sum of `stream` or of `active` on one device may be relied on, other than what follows from the above.
Results may differ from the reference program's by a relative error of at most 0.001.
Values sent between devices are 32-bit elements; how exact they have to be, the bound alone decides.
A program may use at most 64 MiB of HBM per device.

```python
import math
import jax
import jax.numpy as jnp

NL = 16
EVENTS = 4
SR = 2048
SC = 4096
AR = 256
AC = 512


def with_ends(values, own_key, least, largest):
    longest = values.shape.index(max(values.shape))
    spots = []
    for shift in (0, 1):
        where = [jax.random.randint(jax.random.fold_in(own_key, axis), (), 0, length) for axis, length in enumerate(values.shape)]
        where[longest] = (where[longest] + shift) % values.shape[longest]
        spots.append(tuple(where))
    return values.at[spots[0]].set(least).at[spots[1]].set(largest)


def block_levels(stream_key, shape, shards, low, top_value):
    factor_of = 1.0
    for axis_at, parts in shards:
        heights = jax.random.uniform(jax.random.fold_in(jax.random.fold_in(stream_key, 6), axis_at), (parts,), jnp.float32, low / len(shards), top_value / len(shards))
        factor_of = factor_of * jnp.repeat(jnp.exp(heights), shape[axis_at] // parts).reshape((-1,) + (1,) * (len(shape) - 1 - axis_at))
    return factor_of


def bell_draw(rng, extent, spread, bound, pieces=(), dtype=jnp.bfloat16):
    array = spread * jax.random.normal(rng, extent, jnp.float32)
    if pieces:
        array = array * block_levels(rng, extent, pieces, -0.22, 0.18)
    return jnp.clip(array, -bound, bound).astype(dtype)


def setup_inputs(seed: int = 0) -> dict:
    splits = jax.random.split(jax.random.key(seed), 12)
    surf_depth = jnp.clip(0.019897461 + 0.17932129 * jax.random.uniform(splits[0], (EVENTS, SR, SC), jnp.float32) ** block_levels(splits[0], (EVENTS, SR, SC), ((0, 4), (1, 128)), -0.2, 0.2), 0.019897461, 0.19921875).astype(jnp.bfloat16)
    surf_mid = jnp.clip(0.019897461 + 0.17932129 * jax.random.uniform(splits[1], (EVENTS, SR, SC), jnp.float32) ** block_levels(splits[1], (EVENTS, SR, SC), ((0, 4), (1, 128)), -0.2, 0.2), 0.019897461, 0.19921875).astype(jnp.bfloat16)
    surf_seed = bell_draw(splits[2], (EVENTS, SR, SC), 1.0, 6.0, ((0, 4), (1, 128)))
    stream = with_ends((jax.random.randint(splits[3], (SR, SC), 0, 5) < 1).astype(jnp.int32), jax.random.fold_in(splits[3], 1), 0, 1)
    infil = jnp.clip(jnp.exp(math.log(0.4) - 2.0794415 * jax.random.uniform(splits[4], (AR, AC), jnp.float32) ** block_levels(splits[4], (AR, AC), ((0, 128),), -0.2, 0.2)), 0.05, 0.4)
    diffus = jnp.clip(0.03 + 0.089999998 * jax.random.uniform(splits[5], (AR, AC), jnp.float32) ** block_levels(splits[5], (AR, AC), ((0, 128),), -0.2, 0.2), 0.03, 0.12)
    leakance = jnp.clip(jnp.exp(math.log(0.05) - 2.3025851 * jax.random.uniform(splits[6], (AC, AR), jnp.float32) ** block_levels(splits[6], (AC, AR), ((0, 128),), -0.2, 0.2)), 0.005, 0.05)
    active = with_ends((jax.random.randint(splits[7], (AC, AR), 0, 8) < 7).astype(jnp.int32), jax.random.fold_in(splits[7], 1), 0, 1)
    jacobi_coef = jnp.clip(0.1 + 0.059999995 * jax.random.uniform(splits[8], (NL, AC, AR), jnp.float32) ** block_levels(splits[8], (NL, AC, AR), ((1, 128),), -0.2, 0.2), 0.1, 0.16)
    head_seed = bell_draw(splits[9], (EVENTS, NL, AC, AR), 1.0, 6.0, ((0, 4), (2, 128)), jnp.float32)
    top_head = bell_draw(splits[10], (EVENTS, AC, AR), 0.1, 0.6, ((0, 4), (1, 128)), jnp.float32)
    return {"surf_depth": surf_depth, "surf_mid": surf_mid, "surf_seed": surf_seed, "stream": stream, "infil": infil, "diffus": diffus, "leakance": leakance, "active": active, "jacobi_coef": jacobi_coef, "head_seed": head_seed, "top_head": top_head}


def laplace_rows(extended):
    center = extended[..., 1:-1, :]
    widened = jnp.pad(center, [(0, 0)] * (center.ndim - 1) + [(1, 1)])
    return extended[..., 2:, :] + extended[..., :-2, :] + widened[..., 2:] + widened[..., :-2] - 4.0 * center


def laplace(field):
    extended = jnp.pad(field, [(0, 0)] * (field.ndim - 2) + [(1, 1), (0, 0)])
    return laplace_rows(extended)


def neighbours_cols(extended):
    center = extended[..., 1:-1, :]
    layered = jnp.pad(center, [(0, 0)] * (center.ndim - 3) + [(1, 1), (0, 0), (0, 0)])
    rowwise = jnp.pad(center, [(0, 0)] * (center.ndim - 1) + [(1, 1)])
    return (extended[..., 2:, :] + extended[..., :-2, :] + rowwise[..., 2:] + rowwise[..., :-2]
            + layered[..., 2:, :, :] + layered[..., :-2, :, :])


def neighbours(field):
    return neighbours_cols(jnp.pad(field, ((0, 0), (1, 1), (0, 0))))


def restrict_sum(field):
    shape = field.shape
    blocks = field.reshape(shape[:-2] + (shape[-2] // 8, 8, shape[-1] // 8, 8))
    return jnp.sum(blocks, axis=(-3, -1))


def prolong(coarse):
    shape = coarse.shape
    wide = jnp.broadcast_to(coarse[..., :, None, :, None], shape[:-2] + (shape[-2], 8, shape[-1], 8))
    return wide.reshape(shape[:-2] + (shape[-2] * 8, shape[-1] * 8))


def reference(surf_depth, surf_mid, surf_seed, stream, infil, diffus, leakance, active, jacobi_coef, head_seed, top_head):
    factor = 1.0 + stream.astype(jnp.float32)
    infil_fine = prolong(infil) * factor
    diff_fine = prolong(diffus) * factor
    coeffs = active.astype(jnp.float32)[None] * jacobi_coef
    depth_list = []
    head_list = []
    charge_list = []
    grad_w = jnp.zeros((AR, AC), jnp.float32)
    grad_g = jnp.zeros((AR, AC), jnp.float32)
    grad_lk = jnp.zeros((AC, AR), jnp.float32)
    for event in range(EVENTS):
        adj_two = surf_seed[event].astype(jnp.float32)
        adj_one = adj_two + laplace(diff_fine * adj_two)
        adj_zero = adj_one + laplace(diff_fine * adj_one)
        leak_cols = restrict_sum(factor * (adj_one + adj_two)).T
        head_two = head_seed[event].at[0].add(leakance * leak_cols)
        weighted = coeffs * head_two
        head_one = neighbours(weighted)
        weighted_next = coeffs * head_one
        head_list.append(neighbours(weighted_next))
        charge = weighted[0] + weighted_next[0]
        charge_list.append(charge)
        source_adj = -adj_zero + prolong(charge.T)
        depth_list.append((adj_zero + infil_fine * source_adj).astype(jnp.bfloat16))
        depth = surf_depth[event].astype(jnp.float32)
        middle = surf_mid[event].astype(jnp.float32)
        start = depth - infil_fine * depth
        grad_w = grad_w + restrict_sum(factor * depth * source_adj)
        grad_g = grad_g + restrict_sum(factor * (adj_two * laplace(middle) + adj_one * laplace(start)))
        grad_lk = grad_lk + top_head[event] * leak_cols
    return (jnp.stack(depth_list), jnp.stack(head_list), jnp.stack(charge_list), grad_w, grad_g, grad_lk)
```

```python
import functools

import jax
import jax.numpy as jnp
from jax import lax
from jax.experimental import pallas as pl
from jax.experimental.pallas import tpu as pltpu
from jax.sharding import PartitionSpec as P

MESH = pl.DeviceIdType.MESH
F32 = jnp.float32
BF16 = jnp.bfloat16
TILES, EVENTS = 128, 4
ROWS, COLS = 16, 4096
LAYERS, OWN, AROWS, ACOLS = 16, 4, 256, 512
NEAR = (0, 1, 15, 8, 7, 9, 6, 10, 5, 11, 4, 12, 3, 13, 2, 14)
FAR = (8, 7, 9, 6, 10, 5, 11, 4, 12, 3, 13, 2, 14, 1, 15, 0)
PLANE = ((2, 1), (2, 0), (1, 1), (3, 1), (1, 0), (3, 0), (0, 1), (0, 0))


def iota(shape, dim):
    return lax.broadcasted_iota(jnp.int32, shape, dim)


def lanes_by(field, shift):
    n = field.shape[-1]
    lane = iota(field.shape, field.ndim - 1)
    inside = lane >= shift if shift > 0 else lane < n + shift
    return jnp.where(inside, pltpu.roll(field, shift % n, axis=field.ndim - 1), 0.0)


def laplace_inner(field):
    row = iota(field.shape, 0)
    above = jnp.where(row == 0, 0.0, pltpu.roll(field, 1, axis=0))
    below = jnp.where(row == ROWS - 1, 0.0, pltpu.roll(field, ROWS - 1, axis=0))
    return below + above + lanes_by(field, -1) + lanes_by(field, 1) - 4.0 * field


def edges(top, bottom):
    row = iota((ROWS, top.shape[-1]), 0)
    return jnp.where(row == 0, top, 0.0) + jnp.where(row == ROWS - 1, bottom, 0.0)


def pieces(values, axis):
    high = values.astype(BF16).astype(F32)
    return jnp.concatenate([high, values - high], axis=axis).astype(BF16)


def compress(field, block_ref):
    n = field.shape[0]
    wide = jnp.concatenate([field[:, q * 1024 : (q + 1) * 1024] for q in range(4)], axis=0)
    out = jnp.dot(pieces(wide, 0), block_ref[...], preferred_element_type=F32)
    out = out[: 4 * n] + out[4 * n :]
    return jnp.concatenate([out[q * n : (q + 1) * n] for q in range(4)], axis=1)


def block_sums(field, block_ref):
    part = compress(field, block_ref)
    return jnp.concatenate(
        [jnp.sum(part[:8], axis=0, keepdims=True), jnp.sum(part[8:], axis=0, keepdims=True)], axis=0
    )


def prolong(coarse):
    halves = []
    spot = iota((8, 128), 1) // 8
    for r in range(2):
        parts = []
        for m in range(COLS // 128):
            q, s = divmod(m, 8)
            source = jnp.broadcast_to(coarse[r : r + 1, q * 128 : (q + 1) * 128], (8, 128))
            parts.append(
                jnp.take_along_axis(source, spot + 16 * s, axis=1, mode="promise_in_bounds")
            )
        halves.append(jnp.concatenate(parts, axis=1))
    return jnp.concatenate(halves, axis=0)


def pad_rows(rows, n):
    return jnp.concatenate([rows, jnp.zeros((n - rows.shape[0], rows.shape[1]), F32)], axis=0)


def neighbours4(field):
    dim = field.ndim - 2
    return (
        pltpu.roll(field, 7, axis=dim)
        + pltpu.roll(field, 1, axis=dim)
        + lanes_by(field, -1)
        + lanes_by(field, 1)
    )


def step_kernel(
    seed_h, stream_h, diffus_h, jac_h, act_h, leak_h, head_h, infil_h, depth_h, mid_h, top_h,
    depth_o, head_o, charge_o, gw_o, gg_o, glk_o,
    seed_v, stream_v, diffus_v, jac_v, act_v, leak_v, head_v, infil_v, depth_v, mid_v, top_v,
    factor, diff, fluxes, adj1, scaled, startv, block_w,
    fs, fr, hs, hr, ls, lr, cw, xs, ms, mr, ns, nr, ev1, ev2,
    in_sem, edge_send, edge_recv, a2a_send, a2a_recv, ev_send, ev_recv,
):
    e = lax.axis_index("event")
    t = lax.axis_index("tile")
    y, z, x = t // 32, (t // 2) % 16, t % 2
    below, above = (t + 1) % TILES, (t + TILES - 1) % TILES
    has_below, has_above = t < TILES - 1, t > 0

    def each_tile(order, act):
        def body(i, carry):
            h = (i + 1) // 2
            dz = order(i, h)
            for dy, dx in PLANE:
                act((((y + dy) % 4) * 16 + (z + dz) % 16) * 2 + (x + dx) % 2)
            return carry

        lax.fori_loop(0, 15, body, 0)
        for dy, dx in PLANE:
            if dy or dx:
                act((((y + dy) % 4) * 16 + z) * 2 + (x + dx) % 2)

    def far_first(i, h):
        return jnp.where(i % 2 == 1, 8 - h, 8 + h)

    loads = [
        pltpu.make_async_copy(src, dst, in_sem.at[n])
        for n, (src, dst) in enumerate(
            zip(
                (seed_h, stream_h, diffus_h, jac_h, act_h, leak_h, head_h, infil_h, depth_h, mid_h, top_h),
                (seed_v, stream_v, diffus_v, jac_v, act_v, leak_v, head_v, infil_v, depth_v, mid_v, top_v),
            )
        )
    ]
    for load in loads:
        load.start()

    barrier = pltpu.get_barrier_semaphore()
    for k in range(1, EVENTS):
        pl.semaphore_signal(barrier, inc=1, device_id=((e + k) % EVENTS, t), device_id_type=MESH)
    each_tile(
        far_first,
        lambda d: pl.semaphore_signal(barrier, inc=1, device_id=(e, d), device_id_type=MESH),
    )

    for load in loads:
        load.wait()

    block_w[...] = (iota((1024, 128), 0) // 8 == iota((1024, 128), 1)).astype(F32).astype(BF16)
    ns[...] = jnp.zeros((TILES, 128), F32)
    ms[...] = jnp.zeros((TILES, 128), F32)
    factor[...] = 1.0 + stream_v[...].astype(F32)
    diff[...] = prolong(diffus_v[...]) * factor[...]
    seed = seed_v[...].astype(F32)
    fluxes[...] = diff[...] * seed
    fs[0] = fluxes[0:1, :]
    fs[1] = fluxes[ROWS - 1 : ROWS, :]
    adj1[...] = seed + laplace_inner(fluxes[...])
    leak_part = block_sums(factor[...] * (adj1[...] + seed), block_w)
    scaled[...] = diff[...] * adj1[...]
    infil_fine = prolong(infil_v[...]) * factor[...]
    depth = depth_v[...].astype(F32)
    startv[...] = depth - infil_fine * depth
    middle = mid_v[...].astype(F32)
    for way, at in ((0, 0), (1, ROWS - 1)):
        hs[way, 0:1, :] = factor[at : at + 1, :]
        hs[way, 1:2, :] = scaled[at : at + 1, :]
        hs[way, 2:3, :] = diff[at : at + 1, :]
        hs[way, 3:4, :] = startv[at : at + 1, :]
        hs[way, 4:5, :] = middle[at : at + 1, :]
        ls[way] = leak_part[way : way + 1]

    coeffs = act_v[...].astype(F32)[None] * jac_v[...]
    weighted = coeffs * head_v[...]
    leak_coef = coeffs[0] * leak_v[...]
    cw[0:LAYERS, 0:OWN, :] = coeffs
    cw[LAYERS : 2 * LAYERS, 0:OWN, :] = weighted
    cw[2 * LAYERS, 0:OWN, :] = leak_coef
    for k, part in enumerate((weighted[0], leak_coef, coeffs[0], weighted[1])):
        for r in range(4):
            moved = part if r == 1 else lanes_by(part, 1 - r)
            xs[pl.ds(k * 4 + r, 4, stride=16), :] = moved[:, :128]
            xs[pl.ds(64 + k * 4 + r, 4, stride=16), :] = moved[:, 128:]
    pick = (iota((TILES, AROWS), 1) == 2 * iota((TILES, AROWS), 0)).astype(F32).astype(BF16)
    ms[:, 0:64] = lax.dot_general(
        jnp.concatenate([pick, pick], axis=1),
        pieces(jnp.concatenate([xs[0:64, :], xs[64:128, :]], axis=1), 1),
        (((1,), (1,)), ((), ())),
        preferred_element_type=F32,
    )

    pl.semaphore_wait(barrier, TILES - 1 + EVENTS - 1)

    def edge_copy(n, src, dst, target):
        return pltpu.make_async_remote_copy(
            src_ref=src,
            dst_ref=dst,
            send_sem=edge_send.at[n],
            recv_sem=edge_recv.at[n],
            device_id=(e, target),
            device_id_type=MESH,
        )

    flux_copies = [edge_copy(0, fs.at[0], fr.at[0], above), edge_copy(1, fs.at[1], fr.at[1], below)]
    leak_copies = [edge_copy(2, ls.at[0], lr.at[0], above), edge_copy(3, ls.at[1], lr.at[1], below)]
    bulk_copies = [edge_copy(4, hs.at[0], hr.at[0], above), edge_copy(5, hs.at[1], hr.at[1], below)]
    head_copies = [
        edge_copy(6, cw.at[:, pl.ds(0, 2), :], cw.at[:, pl.ds(4, 2), :], above),
        edge_copy(7, cw.at[:, pl.ds(2, 2), :], cw.at[:, pl.ds(6, 2), :], below),
    ]
    for copy in flux_copies + leak_copies + bulk_copies:
        copy.start()

    def to_owner(n, src, dst):
        def act(d):
            pltpu.make_async_remote_copy(
                src_ref=src.at[pl.ds(d, 1)],
                dst_ref=dst.at[pl.ds(t, 1)],
                send_sem=a2a_send.at[n],
                recv_sem=a2a_recv.at[n],
                device_id=(e, d),
                device_id_type=MESH,
            ).start()

        return act

    def all_of(n, src, dst):
        return pltpu.make_async_remote_copy(
            src_ref=src.at[pl.ds(0, TILES - 1)],
            dst_ref=dst.at[pl.ds(0, TILES - 1)],
            send_sem=a2a_send.at[n],
            recv_sem=a2a_recv.at[n],
            device_id=(e, below),
            device_id_type=MESH,
        )

    mr[pl.ds(t, 1), :] = ms[pl.ds(t, 1), :]
    each_tile(far_first, to_owner(0, ms, mr))
    for copy in head_copies:
        copy.start()

    for copy in flux_copies:
        copy.wait()
    flux_below = jnp.where(has_below, fr[0], 0.0)
    flux_above = jnp.where(has_above, fr[1], 0.0)
    own_edges = compress(
        pad_rows(
            jnp.concatenate(
                [factor[0:1, :] * flux_above, factor[ROWS - 1 : ROWS, :] * flux_below], axis=0
            ),
            8,
        ),
        block_w,
    )
    leak_own = leak_part + own_edges[0:2]
    wide = jnp.concatenate(
        [lanes_by(leak_own, -c) if c else leak_own for c in (0, 1, 2, 3, 4, 5, -2, -1)], axis=0
    )
    every = (iota((TILES, ACOLS), 1) == 4 * iota((TILES, ACOLS), 0)).astype(F32).astype(BF16)
    ns[:, 0:16] = lax.dot_general(
        jnp.concatenate([every, every], axis=1),
        pieces(wide, 1),
        (((1,), (1,)), ((), ())),
        preferred_element_type=F32,
    )
    nr[pl.ds(t, 1), :] = ns[pl.ds(t, 1), :]
    each_tile(far_first, to_owner(1, ns, nr))

    adj1[...] = adj1[...] + edges(flux_above, flux_below)
    for copy in leak_copies + bulk_copies:
        copy.wait()

    def outer(n):
        return (
            jnp.where(has_above, hr[1, n : n + 1, :], 0.0),
            jnp.where(has_below, hr[0, n : n + 1, :], 0.0),
        )

    first, last = fluxes[0:1, :], fluxes[ROWS - 1 : ROWS, :]
    factor_above, factor_below = outer(0)
    scaled_above, scaled_below = outer(1)
    diff_above, diff_below = outer(2)
    next_above = scaled_above + diff_above * first
    next_below = scaled_below + diff_below * last
    other_edges = compress(
        pad_rows(jnp.concatenate([factor_above * first, factor_below * last], axis=0), 8), block_w
    )
    leak_above = jnp.where(has_above, lr[1], 0.0) + other_edges[0:1]
    leak_below = jnp.where(has_below, lr[0], 0.0) + other_edges[1:2]
    adj_zero = (
        adj1[...] + laplace_inner(diff[...] * adj1[...]) + edges(next_above, next_below)
    )
    lap_mid = laplace_inner(mid_v[...].astype(F32)) + edges(*outer(4))
    lap_start = laplace_inner(startv[...]) + edges(*outer(3))
    local_g = block_sums(
        factor[...] * (seed_v[...].astype(F32) * lap_mid + adj1[...] * lap_start), block_w
    )

    all_of(0, ms, mr).wait()
    turned = mr[...].T[0:64]
    spread = (iota((TILES, ACOLS), 1) // 4 == iota((TILES, ACOLS), 0)).astype(F32).astype(BF16)
    copied = jnp.dot(pieces(turned, 0), spread, preferred_element_type=F32)
    copied = copied[0:64] + copied[64:128]
    col = iota((16, ACOLS), 1) % 4
    coarse = jnp.zeros((16, ACOLS), F32)
    for c in range(4):
        coarse = jnp.where(col == c, copied[16 * c : 16 * c + 16], coarse)
    w_zero = coarse[0:4] + coarse[4:8] * jnp.concatenate([leak_above, leak_own, leak_below], axis=0)
    mid_w = w_zero[1:3]
    around = lanes_by(mid_w, 1) + lanes_by(mid_w, -1) + w_zero[0:2] + w_zero[2:4] + coarse[13:15]
    recharge = mid_w + coarse[9:11] * around
    source = prolong(recharge) - adj_zero
    infil_again = prolong(infil_v[...]) * factor[...]
    depth_o[...] = (adj_zero + infil_again * source).astype(BF16)
    local_w = block_sums(factor[...] * depth_v[...].astype(F32) * source, block_w)

    def event_copies(n, buf):
        return [
            pltpu.make_async_remote_copy(
                src_ref=buf.at[e],
                dst_ref=buf.at[e],
                send_sem=ev_send.at[n, k],
                recv_sem=ev_recv.at[n, k],
                device_id=((e + k) % EVENTS, t),
                device_id_type=MESH,
            )
            for k in range(1, EVENTS)
        ]

    ev1[e] = jnp.concatenate([local_w, local_g], axis=0)
    grad_copies = event_copies(0, ev1)
    for copy in grad_copies:
        copy.start()

    for copy in head_copies:
        copy.wait()
    slot = iota((8, AROWS), 0)
    column = OWN * t + slot - jnp.where(slot < 6, 0, 8)
    known = jnp.where((column >= 0) & (column < ACOLS), 1.0, 0.0)
    c_all = cw[0:LAYERS] * known[None]
    w_all = cw[LAYERS : 2 * LAYERS] * known[None]
    lk_all = cw[2 * LAYERS] * known
    blank = jnp.zeros((1, 8, AROWS), F32)

    def layered(field):
        return jnp.concatenate([field[1:], blank], axis=0) + jnp.concatenate(
            [blank, field[:-1]], axis=0
        )

    w_next = c_all * (neighbours4(w_all) + layered(w_all))
    base = (neighbours4(w_next) + layered(w_next))[:, 0:OWN, :]
    head_o[3:LAYERS] = base[3:LAYERS]

    all_of(1, ns, nr).wait()
    xs[...] = nr[...].T
    both = jnp.concatenate([xs[pl.ds(0, 8, stride=2), :], xs[pl.ds(1, 8, stride=2), :]], axis=1)
    half, spot = iota((256, AROWS), 0), iota((256, AROWS), 1)
    place = (spot == 2 * (half % TILES) + half // TILES).astype(F32).astype(BF16)
    leak = jnp.dot(pieces(both, 0), place, preferred_element_type=F32)
    leak = leak[0:8] + leak[8:16]
    ev2[e] = top_v[...] * leak[0:OWN]
    lk_copies = event_copies(1, ev2)
    for copy in lk_copies:
        copy.start()
    more_w = lk_all * leak
    next_zero = c_all[0] * neighbours4(more_w)
    next_one = c_all[1] * more_w
    charge_o[...] = (w_all[0] + w_next[0] + more_w + next_zero)[0:OWN]
    head_o[0] = base[0] + (neighbours4(next_zero) + next_one)[0:OWN]
    head_o[1] = base[1] + (next_zero + neighbours4(next_one))[0:OWN]
    head_o[2] = base[2] + next_one[0:OWN]

    for copy in grad_copies:
        copy.wait()
    total = ev1[0] + ev1[1] + ev1[2] + ev1[3]
    gw_o[...] = total[0:2]
    gg_o[...] = total[2:4]
    for copy in lk_copies:
        copy.wait()
    glk_o[...] = ev2[0] + ev2[1] + ev2[2] + ev2[3]


def hand_over(*refs):
    half = len(refs) // 2
    for source, target in zip(refs[:half], refs[half:]):
        target[...] = source[...]


def per_device(
    surf_depth, surf_mid, surf_seed, stream, infil, diffus, leakance, active, jacobi_coef, head_seed, top_head
):
    args = (
        surf_seed[0], stream, diffus, jacobi_coef, active, leakance, head_seed[0], infil,
        surf_depth[0], surf_mid[0], top_head[0],
    )
    outs = [
        jax.ShapeDtypeStruct(shape, dtype)
        for shape, dtype in (
            ((ROWS, COLS), BF16),
            ((LAYERS, OWN, AROWS), F32),
            ((OWN, AROWS), F32),
            ((2, ACOLS), F32),
            ((2, ACOLS), F32),
            ((OWN, AROWS), F32),
        )
    ]
    vmem = pl.BlockSpec(memory_space=pltpu.VMEM)
    hbm = pl.BlockSpec(memory_space=pltpu.HBM)
    field = pltpu.VMEM((ROWS, COLS), F32)
    results = pl.pallas_call(
        step_kernel,
        out_shape=outs,
        in_specs=[hbm] * len(args),
        out_specs=[vmem] * len(outs),
        scratch_shapes=[pltpu.VMEM(a.shape, a.dtype) for a in args]
        + [field] * 6
        + [
            pltpu.VMEM((1024, 128), BF16),
            pltpu.VMEM((2, 1, COLS), F32),
            pltpu.VMEM((2, 1, COLS), F32),
            pltpu.VMEM((2, 5, COLS), F32),
            pltpu.VMEM((2, 5, COLS), F32),
            pltpu.VMEM((2, 1, ACOLS), F32),
            pltpu.VMEM((2, 1, ACOLS), F32),
            pltpu.VMEM((2 * LAYERS + 1, 8, AROWS), F32),
            pltpu.VMEM((128, 128), F32),
            pltpu.VMEM((TILES, 128), F32),
            pltpu.VMEM((TILES, 128), F32),
            pltpu.VMEM((TILES, 128), F32),
            pltpu.VMEM((TILES, 128), F32),
            pltpu.VMEM((EVENTS, 4, ACOLS), F32),
            pltpu.VMEM((EVENTS, OWN, AROWS), F32),
            pltpu.SemaphoreType.DMA((len(args),)),
            pltpu.SemaphoreType.DMA((8,)),
            pltpu.SemaphoreType.DMA((8,)),
            pltpu.SemaphoreType.DMA((2,)),
            pltpu.SemaphoreType.DMA((2,)),
            pltpu.SemaphoreType.DMA((2, EVENTS)),
            pltpu.SemaphoreType.DMA((2, EVENTS)),
        ],
        compiler_params=pltpu.CompilerParams(
            collective_id=0, has_side_effects=True, vmem_limit_bytes=63 * 1024 * 1024
        ),
    )(*args)
    depth, head, charge, grad_w, grad_g, grad_lk = pl.pallas_call(
        hand_over, out_shape=outs, in_specs=[vmem] * len(outs), out_specs=[vmem] * len(outs)
    )(*results)
    return depth[None], head[None], charge[None], grad_w, grad_g, grad_lk


def solution(mesh):
    return jax.shard_map(
        per_device,
        mesh=mesh,
        in_specs=(
            P("event", "tile", None),
            P("event", "tile", None),
            P("event", "tile", None),
            P("tile", None),
            P("tile", None),
            P("tile", None),
            P("tile", None),
            P("tile", None),
            P(None, "tile", None),
            P("event", None, "tile", None),
            P("event", "tile", None),
        ),
        out_specs=(
            P("event", "tile", None),
            P("event", None, "tile", None),
            P("event", "tile", None),
            P("tile", None),
            P("tile", None),
            P("tile", None),
        ),
        check_vma=False,
    )
```

```python
import functools

import jax
import jax.numpy as jnp
from jax import lax
from jax.experimental import pallas as pl
from jax.experimental.pallas import tpu as pltpu
from jax.sharding import PartitionSpec as P

MESH = pl.DeviceIdType.MESH
F32 = jnp.float32
BF16 = jnp.bfloat16
TILES, EVENTS = 128, 4
ROWS, COLS = 16, 4096
LAYERS, OWN, AROWS, ACOLS = 16, 4, 256, 512
NEAR = (0, 1, 15, 8, 7, 9, 6, 10, 5, 11, 4, 12, 3, 13, 2, 14)
FAR = (8, 7, 9, 6, 10, 5, 11, 4, 12, 3, 13, 2, 14, 1, 15, 0)
PLANE = ((2, 1), (2, 0), (1, 1), (3, 1), (1, 0), (3, 0), (0, 1), (0, 0))


def iota(shape, dim):
    return lax.broadcasted_iota(jnp.int32, shape, dim)


def lanes_by(field, shift):
    n = field.shape[-1]
    lane = iota(field.shape, field.ndim - 1)
    inside = lane >= shift if shift > 0 else lane < n + shift
    return jnp.where(inside, pltpu.roll(field, shift % n, axis=field.ndim - 1), 0.0)


def laplace_inner(field):
    row = iota(field.shape, 0)
    above = jnp.where(row == 0, 0.0, pltpu.roll(field, 1, axis=0))
    below = jnp.where(row == ROWS - 1, 0.0, pltpu.roll(field, ROWS - 1, axis=0))
    return below + above + lanes_by(field, -1) + lanes_by(field, 1) - 4.0 * field


def edges(top, bottom):
    row = iota((ROWS, top.shape[-1]), 0)
    return jnp.where(row == 0, top, 0.0) + jnp.where(row == ROWS - 1, bottom, 0.0)


def pieces(values, axis):
    high = values.astype(BF16).astype(F32)
    return jnp.concatenate([high, values - high], axis=axis).astype(BF16)


def compress(field, block_ref):
    n = field.shape[0]
    wide = jnp.concatenate([field[:, q * 1024 : (q + 1) * 1024] for q in range(4)], axis=0)
    out = jnp.dot(pieces(wide, 0), block_ref[...], preferred_element_type=F32)
    out = out[: 4 * n] + out[4 * n :]
    return jnp.concatenate([out[q * n : (q + 1) * n] for q in range(4)], axis=1)


def block_sums(field, block_ref):
    part = compress(field, block_ref)
    return jnp.concatenate(
        [jnp.sum(part[:8], axis=0, keepdims=True), jnp.sum(part[8:], axis=0, keepdims=True)], axis=0
    )


def prolong(coarse):
    halves = []
    spot = iota((8, 128), 1) // 8
    for r in range(2):
        parts = []
        for m in range(COLS // 128):
            q, s = divmod(m, 8)
            source = jnp.broadcast_to(coarse[r : r + 1, q * 128 : (q + 1) * 128], (8, 128))
            parts.append(
                jnp.take_along_axis(source, spot + 16 * s, axis=1, mode="promise_in_bounds")
            )
        halves.append(jnp.concatenate(parts, axis=1))
    return jnp.concatenate(halves, axis=0)


def prolong_rows(coarse):
    spot = iota((8, 128), 1) // 8
    return jnp.concatenate(
        [
            jnp.take_along_axis(
                coarse[:, (m // 8) * 128 : (m // 8 + 1) * 128],
                spot + 16 * (m % 8),
                axis=1,
                mode="promise_in_bounds",
            )
            for m in range(COLS // 128)
        ],
        axis=1,
    )


def pad_rows(rows, n):
    return jnp.concatenate([rows, jnp.zeros((n - rows.shape[0], rows.shape[1]), F32)], axis=0)


def neighbours4(field):
    dim = field.ndim - 2
    return (
        pltpu.roll(field, 7, axis=dim)
        + pltpu.roll(field, 1, axis=dim)
        + lanes_by(field, -1)
        + lanes_by(field, 1)
    )


def step_kernel(
    seed_h, stream_h, diffus_h, jac_h, act_h, leak_h, head_h, infil_h, depth_h, mid_h, top_h,
    depth_o, head_o, charge_o, gw_o, gg_o, glk_o,
    seed_v, stream_v, diffus_v, jac_v, act_v, leak_v, head_v, infil_v, depth_v, mid_v, top_v,
    factor, diff, fluxes, adj1, scaled, startv, infilf, block_w,
    fs, fr, hs, hr, gs, gr, ls, lr, cw, xs, ms, mr, ns, nr, ev1, ev2,
    in_sem, edge_send, edge_recv, a2a_send, a2a_recv, ev_send, ev_recv,
):
    e = lax.axis_index("event")
    t = lax.axis_index("tile")
    y, z, x = t // 32, (t // 2) % 16, t % 2
    below, above = (t + 1) % TILES, (t + TILES - 1) % TILES
    has_below, has_above = t < TILES - 1, t > 0

    def each_tile(order, act):
        def body(i, carry):
            h = (i + 1) // 2
            dz = order(i, h)
            for dy, dx in PLANE:
                act((((y + dy) % 4) * 16 + (z + dz) % 16) * 2 + (x + dx) % 2)
            return carry

        lax.fori_loop(0, 15, body, 0)
        for dy, dx in PLANE:
            if dy or dx:
                act((((y + dy) % 4) * 16 + z) * 2 + (x + dx) % 2)

    def far_first(i, h):
        return jnp.where(i % 2 == 1, 8 - h, 8 + h)

    loads = [
        pltpu.make_async_copy(src, dst, in_sem.at[n])
        for n, (src, dst) in enumerate(
            zip(
                (seed_h, stream_h, diffus_h, jac_h, act_h, leak_h, head_h, infil_h, depth_h, mid_h, top_h),
                (seed_v, stream_v, diffus_v, jac_v, act_v, leak_v, head_v, infil_v, depth_v, mid_v, top_v),
            )
        )
    ]
    for load in loads:
        load.start()

    barrier = pltpu.get_barrier_semaphore()
    for k in range(1, EVENTS):
        pl.semaphore_signal(barrier, inc=1, device_id=((e + k) % EVENTS, t), device_id_type=MESH)
    each_tile(
        far_first,
        lambda d: pl.semaphore_signal(barrier, inc=1, device_id=(e, d), device_id_type=MESH),
    )

    for load in loads:
        load.wait()

    block_w[...] = (iota((1024, 128), 0) // 8 == iota((1024, 128), 1)).astype(F32).astype(BF16)
    ns[...] = jnp.zeros((TILES, 128), F32)
    ms[...] = jnp.zeros((TILES, 128), F32)
    factor[...] = 1.0 + stream_v[...].astype(F32)
    diff[...] = prolong(diffus_v[...]) * factor[...]
    seed = seed_v[...].astype(F32)
    fluxes[...] = diff[...] * seed
    fs[0] = fluxes[0:1, :]
    fs[1] = fluxes[ROWS - 1 : ROWS, :]
    adj1[...] = seed + laplace_inner(fluxes[...])
    leak_part = block_sums(factor[...] * (adj1[...] + seed), block_w)
    scaled[...] = diff[...] * adj1[...]
    infilf[...] = prolong(infil_v[...]) * factor[...]
    depth = depth_v[...].astype(F32)
    startv[...] = depth - infilf[...] * depth
    middle = mid_v[...].astype(F32)
    for way, at in ((0, 0), (1, ROWS - 1)):
        hs[way, 0:1, :] = factor[at : at + 1, :]
        hs[way, 1:2, :] = scaled[at : at + 1, :]
        gs[way, 0:1, :] = startv[at : at + 1, :]
        gs[way, 1:2, :] = middle[at : at + 1, :]
        ls[way, 0:1, :] = leak_part[way : way + 1]
        ls[way, 1:2, :] = diffus_v[way : way + 1, :]

    coeffs = act_v[...].astype(F32)[None] * jac_v[...]
    weighted = coeffs * head_v[...]
    leak_coef = coeffs[0] * leak_v[...]
    cw[0:LAYERS, 0:OWN, :] = coeffs
    cw[LAYERS : 2 * LAYERS, 0:OWN, :] = weighted
    cw[2 * LAYERS, 0:OWN, :] = leak_coef
    for k, part in enumerate((weighted[0], leak_coef, coeffs[0], weighted[1])):
        for r in range(4):
            moved = part if r == 1 else lanes_by(part, 1 - r)
            xs[pl.ds(k * 4 + r, 4, stride=16), :] = moved[:, :128]
            xs[pl.ds(64 + k * 4 + r, 4, stride=16), :] = moved[:, 128:]
    pick = (iota((TILES, AROWS), 1) == 2 * iota((TILES, AROWS), 0)).astype(F32).astype(BF16)
    ms[:, 0:64] = lax.dot_general(
        jnp.concatenate([pick, pick], axis=1),
        pieces(jnp.concatenate([xs[0:64, :], xs[64:128, :]], axis=1), 1),
        (((1,), (1,)), ((), ())),
        preferred_element_type=F32,
    )

    pl.semaphore_wait(barrier, TILES - 1 + EVENTS - 1)

    def edge_copy(n, src, dst, target):
        return pltpu.make_async_remote_copy(
            src_ref=src,
            dst_ref=dst,
            send_sem=edge_send.at[n],
            recv_sem=edge_recv.at[n],
            device_id=(e, target),
            device_id_type=MESH,
        )

    flux_copies = [edge_copy(0, fs.at[0], fr.at[0], above), edge_copy(1, fs.at[1], fr.at[1], below)]
    bulk_copies = [
        edge_copy(2, ls.at[0], lr.at[0], above),
        edge_copy(3, ls.at[1], lr.at[1], below),
        edge_copy(4, hs.at[0], hr.at[0], above),
        edge_copy(5, hs.at[1], hr.at[1], below),
    ]
    late_copies = [edge_copy(6, gs.at[0], gr.at[0], above), edge_copy(7, gs.at[1], gr.at[1], below)]
    heads = pl.ds(LAYERS, LAYERS + 1)
    head_copies = [
        edge_copy(8, cw.at[heads, pl.ds(0, 2), :], cw.at[heads, pl.ds(4, 2), :], above),
        edge_copy(9, cw.at[heads, pl.ds(2, 2), :], cw.at[heads, pl.ds(6, 2), :], below),
        edge_copy(
            10, cw.at[pl.ds(0, LAYERS), pl.ds(0, 1), :], cw.at[pl.ds(0, LAYERS), pl.ds(4, 1), :], above
        ),
        edge_copy(
            11, cw.at[pl.ds(0, LAYERS), pl.ds(3, 1), :], cw.at[pl.ds(0, LAYERS), pl.ds(7, 1), :], below
        ),
    ]
    for copy in flux_copies + bulk_copies:
        copy.start()

    def to_owner(n, src, dst):
        def act(d):
            pltpu.make_async_remote_copy(
                src_ref=src.at[pl.ds(d, 1)],
                dst_ref=dst.at[pl.ds(t, 1)],
                send_sem=a2a_send.at[n],
                recv_sem=a2a_recv.at[n],
                device_id=(e, d),
                device_id_type=MESH,
            ).start()

        return act

    def all_of(n, src, dst):
        return pltpu.make_async_remote_copy(
            src_ref=src.at[pl.ds(0, TILES - 1)],
            dst_ref=dst.at[pl.ds(0, TILES - 1)],
            send_sem=a2a_send.at[n],
            recv_sem=a2a_recv.at[n],
            device_id=(e, below),
            device_id_type=MESH,
        )

    mr[pl.ds(t, 1), :] = ms[pl.ds(t, 1), :]
    each_tile(far_first, to_owner(0, ms, mr))
    for copy in late_copies + head_copies:
        copy.start()

    start_inner = laplace_inner(startv[...])
    start_ends = (start_inner[0:1], start_inner[ROWS - 1 : ROWS])
    part_g = block_sums(
        factor[...]
        * (
            seed_v[...].astype(F32) * laplace_inner(mid_v[...].astype(F32))
            + adj1[...] * start_inner
        ),
        block_w,
    )
    water = block_sums(factor[...] * depth_v[...].astype(F32), block_w)

    for copy in flux_copies:
        copy.wait()
    flux_below = jnp.where(has_below, fr[0], 0.0)
    flux_above = jnp.where(has_above, fr[1], 0.0)
    own_edges = compress(
        pad_rows(
            jnp.concatenate(
                [factor[0:1, :] * flux_above, factor[ROWS - 1 : ROWS, :] * flux_below], axis=0
            ),
            8,
        ),
        block_w,
    )
    leak_own = leak_part + own_edges[0:2]
    wide = jnp.concatenate(
        [lanes_by(leak_own, -c) if c else leak_own for c in (0, 1, 2, 3, 4, 5, -2, -1)], axis=0
    )
    every = (iota((TILES, ACOLS), 1) == 4 * iota((TILES, ACOLS), 0)).astype(F32).astype(BF16)
    ns[:, 0:16] = lax.dot_general(
        jnp.concatenate([every, every], axis=1),
        pieces(wide, 1),
        (((1,), (1,)), ((), ())),
        preferred_element_type=F32,
    )
    nr[pl.ds(t, 1), :] = ns[pl.ds(t, 1), :]
    each_tile(far_first, to_owner(1, ns, nr))

    adj1[...] = adj1[...] + edges(flux_above, flux_below)
    for copy in bulk_copies:
        copy.wait()

    def outer(ref, n):
        return (
            jnp.where(has_above, ref[1, n : n + 1, :], 0.0),
            jnp.where(has_below, ref[0, n : n + 1, :], 0.0),
        )

    first, last = fluxes[0:1, :], fluxes[ROWS - 1 : ROWS, :]
    factor_above, factor_below = outer(hr, 0)
    scaled_above, scaled_below = outer(hr, 1)
    spread_ends = prolong_rows(pad_rows(jnp.concatenate([lr[1, 1:2, :], lr[0, 1:2, :]], axis=0), 8))
    next_above = scaled_above + spread_ends[0:1] * factor_above * first
    next_below = scaled_below + spread_ends[1:2] * factor_below * last
    other_edges = compress(
        pad_rows(jnp.concatenate([factor_above * first, factor_below * last], axis=0), 8), block_w
    )
    leak_above = jnp.where(has_above, lr[1, 0:1, :], 0.0) + other_edges[0:1]
    leak_below = jnp.where(has_below, lr[0, 0:1, :], 0.0) + other_edges[1:2]
    adj_zero = (
        adj1[...] + laplace_inner(diff[...] * adj1[...]) + edges(next_above, next_below)
    )
    scaled[...] = adj_zero
    drained = block_sums(factor[...] * depth_v[...].astype(F32) * adj_zero, block_w)

    all_of(0, ms, mr).wait()
    turned = mr[...].T[0:64]
    spread = (iota((TILES, ACOLS), 1) // 4 == iota((TILES, ACOLS), 0)).astype(F32).astype(BF16)
    copied = jnp.dot(pieces(turned, 0), spread, preferred_element_type=F32)
    copied = copied[0:64] + copied[64:128]
    col = iota((16, ACOLS), 1) % 4
    coarse = jnp.zeros((16, ACOLS), F32)
    for c in range(4):
        coarse = jnp.where(col == c, copied[16 * c : 16 * c + 16], coarse)
    w_zero = coarse[0:4] + coarse[4:8] * jnp.concatenate([leak_above, leak_own, leak_below], axis=0)
    mid_w = w_zero[1:3]
    around = lanes_by(mid_w, 1) + lanes_by(mid_w, -1) + w_zero[0:2] + w_zero[2:4] + coarse[13:15]
    recharge = mid_w + coarse[9:11] * around
    local_w = water * recharge - drained
    for copy in late_copies:
        copy.wait()
    start_above, start_below = outer(gr, 0)
    mid_above, mid_below = outer(gr, 1)
    seed_edges = seed_v[...].astype(F32)
    edge_above = factor[0:1, :] * (
        seed_edges[0:1] * mid_above + flux_above * start_ends[0] + adj1[0:1, :] * start_above
    )
    edge_below = factor[ROWS - 1 : ROWS, :] * (
        seed_edges[ROWS - 1 : ROWS] * mid_below
        + flux_below * start_ends[1]
        + adj1[ROWS - 1 : ROWS, :] * start_below
    )
    edge_g = compress(pad_rows(jnp.concatenate([edge_above, edge_below], axis=0), 8), block_w)
    local_g = part_g + edge_g[0:2]

    def event_copies(n, buf):
        return [
            pltpu.make_async_remote_copy(
                src_ref=buf.at[e],
                dst_ref=buf.at[e],
                send_sem=ev_send.at[n, k],
                recv_sem=ev_recv.at[n, k],
                device_id=((e + k) % EVENTS, t),
                device_id_type=MESH,
            )
            for k in range(1, EVENTS)
        ]

    ev1[e] = jnp.concatenate([local_w, local_g], axis=0)
    grad_copies = event_copies(0, ev1)
    for copy in grad_copies:
        copy.start()

    depth_o[...] = (scaled[...] + infilf[...] * (prolong(recharge) - scaled[...])).astype(BF16)

    for copy in head_copies:
        copy.wait()
    slot = iota((8, AROWS), 0)
    column = OWN * t + slot - jnp.where(slot < 6, 0, 8)
    known = jnp.where((column >= 0) & (column < ACOLS), 1.0, 0.0)
    offset = iota((LAYERS, 8, AROWS), 1)
    c_all = jnp.where((offset == 5) | (offset == 6), 0.0, cw[0:LAYERS]) * known[None]
    w_all = cw[LAYERS : 2 * LAYERS] * known[None]
    lk_all = cw[2 * LAYERS] * known
    blank = jnp.zeros((1, 8, AROWS), F32)

    def layered(field):
        return jnp.concatenate([field[1:], blank], axis=0) + jnp.concatenate(
            [blank, field[:-1]], axis=0
        )

    w_next = c_all * (neighbours4(w_all) + layered(w_all))
    base = (neighbours4(w_next) + layered(w_next))[:, 0:OWN, :]
    head_o[3:LAYERS] = base[3:LAYERS]

    all_of(1, ns, nr).wait()
    xs[...] = nr[...].T
    both = jnp.concatenate([xs[pl.ds(0, 8, stride=2), :], xs[pl.ds(1, 8, stride=2), :]], axis=1)
    half, spot = iota((256, AROWS), 0), iota((256, AROWS), 1)
    place = (spot == 2 * (half % TILES) + half // TILES).astype(F32).astype(BF16)
    leak = jnp.dot(pieces(both, 0), place, preferred_element_type=F32)
    leak = leak[0:8] + leak[8:16]
    ev2[e] = top_v[...] * leak[0:OWN]
    lk_copies = event_copies(1, ev2)
    for copy in lk_copies:
        copy.start()
    more_w = lk_all * leak
    next_zero = c_all[0] * neighbours4(more_w)
    next_one = c_all[1] * more_w
    charge_o[...] = (w_all[0] + w_next[0] + more_w + next_zero)[0:OWN]
    head_o[0] = base[0] + (neighbours4(next_zero) + next_one)[0:OWN]
    head_o[1] = base[1] + (next_zero + neighbours4(next_one))[0:OWN]
    head_o[2] = base[2] + next_one[0:OWN]

    for copy in grad_copies:
        copy.wait()
    total = ev1[0] + ev1[1] + ev1[2] + ev1[3]
    gw_o[...] = total[0:2]
    gg_o[...] = total[2:4]
    for copy in lk_copies:
        copy.wait()
    glk_o[...] = ev2[0] + ev2[1] + ev2[2] + ev2[3]


def hand_over(*refs):
    sem = refs[-1]
    half = len(refs) // 2
    copies = [
        pltpu.make_async_copy(source, target, sem.at[n])
        for n, (source, target) in enumerate(zip(refs[:half], refs[half:-1]))
    ]
    for copy in copies:
        copy.start()
    for copy in copies:
        copy.wait()


def per_device(
    surf_depth, surf_mid, surf_seed, stream, infil, diffus, leakance, active, jacobi_coef, head_seed, top_head
):
    args = (
        surf_seed[0], stream, diffus, jacobi_coef, active, leakance, head_seed[0], infil,
        surf_depth[0], surf_mid[0], top_head[0],
    )
    outs = [
        jax.ShapeDtypeStruct(shape, dtype)
        for shape, dtype in (
            ((ROWS, COLS), BF16),
            ((LAYERS, OWN, AROWS), F32),
            ((OWN, AROWS), F32),
            ((2, ACOLS), F32),
            ((2, ACOLS), F32),
            ((OWN, AROWS), F32),
        )
    ]
    vmem = pl.BlockSpec(memory_space=pltpu.VMEM)
    hbm = pl.BlockSpec(memory_space=pltpu.HBM)
    field = pltpu.VMEM((ROWS, COLS), F32)
    results = pl.pallas_call(
        step_kernel,
        out_shape=outs,
        in_specs=[hbm] * len(args),
        out_specs=[vmem] * len(outs),
        scratch_shapes=[pltpu.VMEM(a.shape, a.dtype) for a in args]
        + [field] * 7
        + [
            pltpu.VMEM((1024, 128), BF16),
            pltpu.VMEM((2, 1, COLS), F32),
            pltpu.VMEM((2, 1, COLS), F32),
            pltpu.VMEM((2, 2, COLS), F32),
            pltpu.VMEM((2, 2, COLS), F32),
            pltpu.VMEM((2, 2, COLS), F32),
            pltpu.VMEM((2, 2, COLS), F32),
            pltpu.VMEM((2, 2, ACOLS), F32),
            pltpu.VMEM((2, 2, ACOLS), F32),
            pltpu.VMEM((2 * LAYERS + 1, 8, AROWS), F32),
            pltpu.VMEM((128, 128), F32),
            pltpu.VMEM((TILES, 128), F32),
            pltpu.VMEM((TILES, 128), F32),
            pltpu.VMEM((TILES, 128), F32),
            pltpu.VMEM((TILES, 128), F32),
            pltpu.VMEM((EVENTS, 4, ACOLS), F32),
            pltpu.VMEM((EVENTS, OWN, AROWS), F32),
            pltpu.SemaphoreType.DMA((len(args),)),
            pltpu.SemaphoreType.DMA((12,)),
            pltpu.SemaphoreType.DMA((12,)),
            pltpu.SemaphoreType.DMA((2,)),
            pltpu.SemaphoreType.DMA((2,)),
            pltpu.SemaphoreType.DMA((2, EVENTS)),
            pltpu.SemaphoreType.DMA((2, EVENTS)),
        ],
        compiler_params=pltpu.CompilerParams(
            collective_id=0, has_side_effects=True, vmem_limit_bytes=40 * 1024 * 1024
        ),
    )(*[pltpu.with_memory_space_constraint(a, pltpu.HBM) for a in args])
    depth, head, charge, grad_w, grad_g, grad_lk = pl.pallas_call(
        hand_over,
        out_shape=outs,
        in_specs=[pl.BlockSpec(memory_space=pl.ANY)] * len(outs),
        out_specs=[hbm] * len(outs),
        scratch_shapes=[pltpu.SemaphoreType.DMA((len(outs),))],
        compiler_params=pltpu.CompilerParams(vmem_limit_bytes=1024 * 1024),
    )(*results)
    return depth[None], head[None], charge[None], grad_w, grad_g, grad_lk


def solution(mesh):
    return jax.shard_map(
        per_device,
        mesh=mesh,
        in_specs=(
            P("event", "tile", None),
            P("event", "tile", None),
            P("event", "tile", None),
            P("tile", None),
            P("tile", None),
            P("tile", None),
            P("tile", None),
            P("tile", None),
            P(None, "tile", None),
            P("event", None, "tile", None),
            P("event", "tile", None),
        ),
        out_specs=(
            P("event", "tile", None),
            P("event", None, "tile", None),
            P("event", "tile", None),
            P("tile", None),
            P("tile", None),
            P("tile", None),
        ),
        check_vma=False,
    )
```

```python
import functools

import jax
import jax.numpy as jnp
from jax import lax
from jax.experimental import pallas as pl
from jax.experimental.pallas import tpu as pltpu
from jax.sharding import PartitionSpec as P

MESH = pl.DeviceIdType.MESH
F32 = jnp.float32
BF16 = jnp.bfloat16
TILES, EVENTS = 128, 4
ROWS, COLS = 16, 4096
LAYERS, OWN, AROWS, ACOLS = 16, 4, 256, 512
NEAR = (0, 1, 15, 8, 7, 9, 6, 10, 5, 11, 4, 12, 3, 13, 2, 14)
FAR = (8, 7, 9, 6, 10, 5, 11, 4, 12, 3, 13, 2, 14, 1, 15, 0)
PLANE = ((2, 1), (2, 0), (1, 1), (3, 1), (1, 0), (3, 0), (0, 1), (0, 0))


def iota(shape, dim):
    return lax.broadcasted_iota(jnp.int32, shape, dim)


def lanes_by(field, shift):
    n = field.shape[-1]
    lane = iota(field.shape, field.ndim - 1)
    inside = lane >= shift if shift > 0 else lane < n + shift
    return jnp.where(inside, pltpu.roll(field, shift % n, axis=field.ndim - 1), 0.0)


def laplace_inner(field):
    row = iota(field.shape, 0)
    above = jnp.where(row == 0, 0.0, pltpu.roll(field, 1, axis=0))
    below = jnp.where(row == ROWS - 1, 0.0, pltpu.roll(field, ROWS - 1, axis=0))
    return below + above + lanes_by(field, -1) + lanes_by(field, 1) - 4.0 * field


def edges(top, bottom):
    row = iota((ROWS, top.shape[-1]), 0)
    return jnp.where(row == 0, top, 0.0) + jnp.where(row == ROWS - 1, bottom, 0.0)


def pieces(values, axis):
    high = values.astype(BF16).astype(F32)
    return jnp.concatenate([high, values - high], axis=axis).astype(BF16)


def compress(field, block_ref):
    n = field.shape[0]
    wide = jnp.concatenate([field[:, q * 1024 : (q + 1) * 1024] for q in range(4)], axis=0)
    out = jnp.dot(pieces(wide, 0), block_ref[...], preferred_element_type=F32)
    out = out[: 4 * n] + out[4 * n :]
    return jnp.concatenate([out[q * n : (q + 1) * n] for q in range(4)], axis=1)


def block_sums(field, block_ref):
    part = compress(field, block_ref)
    return jnp.concatenate(
        [jnp.sum(part[:8], axis=0, keepdims=True), jnp.sum(part[8:], axis=0, keepdims=True)], axis=0
    )


def prolong(coarse):
    halves = []
    spot = iota((8, 128), 1) // 8
    for r in range(2):
        parts = []
        for m in range(COLS // 128):
            q, s = divmod(m, 8)
            source = jnp.broadcast_to(coarse[r : r + 1, q * 128 : (q + 1) * 128], (8, 128))
            parts.append(
                jnp.take_along_axis(source, spot + 16 * s, axis=1, mode="promise_in_bounds")
            )
        halves.append(jnp.concatenate(parts, axis=1))
    return jnp.concatenate(halves, axis=0)


def prolong_rows(coarse):
    spot = iota((8, 128), 1) // 8
    return jnp.concatenate(
        [
            jnp.take_along_axis(
                coarse[:, (m // 8) * 128 : (m // 8 + 1) * 128],
                spot + 16 * (m % 8),
                axis=1,
                mode="promise_in_bounds",
            )
            for m in range(COLS // 128)
        ],
        axis=1,
    )


def pad_rows(rows, n):
    return jnp.concatenate([rows, jnp.zeros((n - rows.shape[0], rows.shape[1]), F32)], axis=0)


def neighbours4(field):
    dim = field.ndim - 2
    return (
        pltpu.roll(field, 7, axis=dim)
        + pltpu.roll(field, 1, axis=dim)
        + lanes_by(field, -1)
        + lanes_by(field, 1)
    )


def step_kernel(
    seed_h, stream_h, diffus_h, jac_h, act_h, leak_h, head_h, infil_h, depth_h, mid_h, top_h,
    depth_o, head_o, charge_o, gw_o, gg_o, glk_o,
    seed_v, stream_v, diffus_v, jac_v, act_v, leak_v, head_v, infil_v, depth_v, mid_v, top_v,
    factor, diff, fluxes, adj1, scaled, startv, infilf, block_w,
    fs, fr, hs, hr, gs, gr, ls, lr, cw, xs, ms, mr, ns, nr, ev1, ev2, every_w, place_w,
    in_sem, edge_send, edge_recv, a2a_send, a2a_recv, ev_send, ev_recv,
):
    e = lax.axis_index("event")
    t = lax.axis_index("tile")
    y, z, x = t // 32, (t // 2) % 16, t % 2
    below, above = (t + 1) % TILES, (t + TILES - 1) % TILES
    has_below, has_above = t < TILES - 1, t > 0

    def each_tile(order, act):
        def body(i, carry):
            h = (i + 1) // 2
            dz = order(i, h)
            for dy, dx in PLANE:
                act((((y + dy) % 4) * 16 + (z + dz) % 16) * 2 + (x + dx) % 2)
            return carry

        lax.fori_loop(0, 15, body, 0)
        for dy, dx in PLANE:
            if dy or dx:
                act((((y + dy) % 4) * 16 + z) * 2 + (x + dx) % 2)

    def far_first(i, h):
        return jnp.where(i % 2 == 1, 8 - h, 8 + h)

    loads = [
        pltpu.make_async_copy(src, dst, in_sem.at[n])
        for n, (src, dst) in enumerate(
            zip(
                (seed_h, stream_h, diffus_h, jac_h, act_h, leak_h, head_h, infil_h, depth_h, mid_h, top_h),
                (seed_v, stream_v, diffus_v, jac_v, act_v, leak_v, head_v, infil_v, depth_v, mid_v, top_v),
            )
        )
    ]
    for load in loads:
        load.start()

    barrier = pltpu.get_barrier_semaphore()
    for near in (above, below):
        pl.semaphore_signal(barrier, inc=1, device_id=(e, near), device_id_type=MESH)
    for k in range(1, EVENTS):
        pl.semaphore_signal(barrier, inc=1, device_id=((e + k) % EVENTS, t), device_id_type=MESH)
    each_tile(
        far_first,
        lambda d: pl.semaphore_signal(barrier, inc=1, device_id=(e, d), device_id_type=MESH),
    )

    for load in loads:
        load.wait()

    block_w[...] = (iota((1024, 128), 0) // 8 == iota((1024, 128), 1)).astype(F32).astype(BF16)
    ns[...] = jnp.zeros((TILES, 128), F32)
    ms[...] = jnp.zeros((TILES, 128), F32)
    factor[...] = 1.0 + stream_v[...].astype(F32)
    diff[...] = prolong(diffus_v[...]) * factor[...]
    seed = seed_v[...].astype(F32)
    fluxes[...] = diff[...] * seed
    fs[0] = fluxes[0:1, :]
    fs[1] = fluxes[ROWS - 1 : ROWS, :]
    adj1[...] = seed + laplace_inner(fluxes[...])
    leak_part = block_sums(factor[...] * (adj1[...] + seed), block_w)
    scaled[...] = diff[...] * adj1[...]
    infilf[...] = prolong(infil_v[...]) * factor[...]
    depth = depth_v[...].astype(F32)
    startv[...] = depth - infilf[...] * depth
    middle = mid_v[...].astype(F32)
    for way, at in ((0, 0), (1, ROWS - 1)):
        hs[way, 0:1, :] = factor[at : at + 1, :]
        hs[way, 1:2, :] = scaled[at : at + 1, :]
        gs[way, 0:1, :] = startv[at : at + 1, :]
        gs[way, 1:2, :] = middle[at : at + 1, :]
        ls[way, 0:1, :] = leak_part[way : way + 1]
        ls[way, 1:2, :] = diffus_v[way : way + 1, :]

    coeffs = act_v[...].astype(F32)[None] * jac_v[...]
    weighted = coeffs * head_v[...]
    leak_coef = coeffs[0] * leak_v[...]
    cw[0:LAYERS, 0:OWN, :] = coeffs
    cw[LAYERS : 2 * LAYERS, 0:OWN, :] = weighted
    cw[2 * LAYERS, 0:OWN, :] = leak_coef
    for k, part in enumerate((weighted[0], leak_coef, coeffs[0], weighted[1])):
        for r in range(4):
            moved = part if r == 1 else lanes_by(part, 1 - r)
            xs[pl.ds(k * 4 + r, 4, stride=16), :] = moved[:, :128]
            xs[pl.ds(64 + k * 4 + r, 4, stride=16), :] = moved[:, 128:]
    pick = (iota((TILES, AROWS), 1) == 2 * iota((TILES, AROWS), 0)).astype(F32).astype(BF16)
    ms[:, 0:64] = lax.dot_general(
        jnp.concatenate([pick, pick], axis=1),
        pieces(jnp.concatenate([xs[0:64, :], xs[64:128, :]], axis=1), 1),
        (((1,), (1,)), ((), ())),
        preferred_element_type=F32,
    )

    pl.semaphore_wait(barrier, TILES - 1 + EVENTS - 1 + 2)

    def edge_copy(n, src, dst, target):
        return pltpu.make_async_remote_copy(
            src_ref=src,
            dst_ref=dst,
            send_sem=edge_send.at[n],
            recv_sem=edge_recv.at[n],
            device_id=(e, target),
            device_id_type=MESH,
        )

    flux_copies = [edge_copy(0, fs.at[0], fr.at[0], above), edge_copy(1, fs.at[1], fr.at[1], below)]
    bulk_copies = [
        edge_copy(2, ls.at[0], lr.at[0], above),
        edge_copy(3, ls.at[1], lr.at[1], below),
        edge_copy(4, hs.at[0], hr.at[0], above),
        edge_copy(5, hs.at[1], hr.at[1], below),
    ]
    late_copies = [edge_copy(6, gs.at[0], gr.at[0], above), edge_copy(7, gs.at[1], gr.at[1], below)]
    heads = pl.ds(LAYERS, LAYERS + 1)
    head_copies = [
        edge_copy(8, cw.at[heads, pl.ds(0, 2), :], cw.at[heads, pl.ds(4, 2), :], above),
        edge_copy(9, cw.at[heads, pl.ds(2, 2), :], cw.at[heads, pl.ds(6, 2), :], below),
        edge_copy(
            10, cw.at[pl.ds(0, LAYERS), pl.ds(0, 1), :], cw.at[pl.ds(0, LAYERS), pl.ds(4, 1), :], above
        ),
        edge_copy(
            11, cw.at[pl.ds(0, LAYERS), pl.ds(3, 1), :], cw.at[pl.ds(0, LAYERS), pl.ds(7, 1), :], below
        ),
    ]
    for copy in flux_copies + bulk_copies:
        copy.start()

    def to_owner(n, src, dst):
        def act(d):
            pltpu.make_async_remote_copy(
                src_ref=src.at[pl.ds(d, 1)],
                dst_ref=dst.at[pl.ds(t, 1)],
                send_sem=a2a_send.at[n],
                recv_sem=a2a_recv.at[n],
                device_id=(e, d),
                device_id_type=MESH,
            ).start()

        return act

    def all_of(n, src, dst):
        return pltpu.make_async_remote_copy(
            src_ref=src.at[pl.ds(0, TILES - 1)],
            dst_ref=dst.at[pl.ds(0, TILES - 1)],
            send_sem=a2a_send.at[n],
            recv_sem=a2a_recv.at[n],
            device_id=(e, below),
            device_id_type=MESH,
        )

    mr[pl.ds(t, 1), :] = ms[pl.ds(t, 1), :]
    each_tile(far_first, to_owner(0, ms, mr))
    for copy in late_copies + head_copies:
        copy.start()

    every = (iota((TILES, ACOLS), 1) == 4 * iota((TILES, ACOLS), 0)).astype(F32).astype(BF16)
    every_w[...] = jnp.concatenate([every, every], axis=1)
    half, spot = iota((256, AROWS), 0), iota((256, AROWS), 1)
    place = (spot == 2 * (half % TILES) + half // TILES).astype(F32).astype(BF16)
    place_w[...] = place

    start_inner = laplace_inner(startv[...])
    start_ends = (start_inner[0:1], start_inner[ROWS - 1 : ROWS])
    part_g = block_sums(
        factor[...]
        * (
            seed_v[...].astype(F32) * laplace_inner(mid_v[...].astype(F32))
            + adj1[...] * start_inner
        ),
        block_w,
    )
    water = block_sums(factor[...] * depth_v[...].astype(F32), block_w)

    for copy in flux_copies:
        copy.wait()
    flux_below = jnp.where(has_below, fr[0], 0.0)
    flux_above = jnp.where(has_above, fr[1], 0.0)
    own_edges = compress(
        pad_rows(
            jnp.concatenate(
                [factor[0:1, :] * flux_above, factor[ROWS - 1 : ROWS, :] * flux_below], axis=0
            ),
            8,
        ),
        block_w,
    )
    leak_own = leak_part + own_edges[0:2]
    wide = jnp.concatenate(
        [lanes_by(leak_own, -c) if c else leak_own for c in (0, 1, 2, 3, 4, 5, -2, -1)], axis=0
    )
    ns[:, 0:16] = lax.dot_general(
        every_w[...],
        pieces(wide, 1),
        (((1,), (1,)), ((), ())),
        preferred_element_type=F32,
    )
    nr[pl.ds(t, 1), :] = ns[pl.ds(t, 1), :]
    each_tile(far_first, to_owner(1, ns, nr))

    adj1[...] = adj1[...] + edges(flux_above, flux_below)
    for copy in bulk_copies:
        copy.wait()

    def outer(ref, n):
        return (
            jnp.where(has_above, ref[1, n : n + 1, :], 0.0),
            jnp.where(has_below, ref[0, n : n + 1, :], 0.0),
        )

    first, last = fluxes[0:1, :], fluxes[ROWS - 1 : ROWS, :]
    factor_above, factor_below = outer(hr, 0)
    scaled_above, scaled_below = outer(hr, 1)
    spread_ends = prolong_rows(pad_rows(jnp.concatenate([lr[1, 1:2, :], lr[0, 1:2, :]], axis=0), 8))
    next_above = scaled_above + spread_ends[0:1] * factor_above * first
    next_below = scaled_below + spread_ends[1:2] * factor_below * last
    other_edges = compress(
        pad_rows(jnp.concatenate([factor_above * first, factor_below * last], axis=0), 8), block_w
    )
    leak_above = jnp.where(has_above, lr[1, 0:1, :], 0.0) + other_edges[0:1]
    leak_below = jnp.where(has_below, lr[0, 0:1, :], 0.0) + other_edges[1:2]
    adj_zero = (
        adj1[...] + laplace_inner(diff[...] * adj1[...]) + edges(next_above, next_below)
    )
    scaled[...] = adj_zero
    drained = block_sums(factor[...] * depth_v[...].astype(F32) * adj_zero, block_w)

    all_of(0, ms, mr).wait()
    turned = mr[...].T[0:64]
    spread = (iota((TILES, ACOLS), 1) // 4 == iota((TILES, ACOLS), 0)).astype(F32).astype(BF16)
    copied = jnp.dot(pieces(turned, 0), spread, preferred_element_type=F32)
    copied = copied[0:64] + copied[64:128]
    col = iota((16, ACOLS), 1) % 4
    coarse = jnp.zeros((16, ACOLS), F32)
    for c in range(4):
        coarse = jnp.where(col == c, copied[16 * c : 16 * c + 16], coarse)
    w_zero = coarse[0:4] + coarse[4:8] * jnp.concatenate([leak_above, leak_own, leak_below], axis=0)
    mid_w = w_zero[1:3]
    around = lanes_by(mid_w, 1) + lanes_by(mid_w, -1) + w_zero[0:2] + w_zero[2:4] + coarse[13:15]
    recharge = mid_w + coarse[9:11] * around
    local_w = water * recharge - drained
    for copy in late_copies:
        copy.wait()
    start_above, start_below = outer(gr, 0)
    mid_above, mid_below = outer(gr, 1)
    seed_edges = seed_v[...].astype(F32)
    edge_above = factor[0:1, :] * (
        seed_edges[0:1] * mid_above + flux_above * start_ends[0] + adj1[0:1, :] * start_above
    )
    edge_below = factor[ROWS - 1 : ROWS, :] * (
        seed_edges[ROWS - 1 : ROWS] * mid_below
        + flux_below * start_ends[1]
        + adj1[ROWS - 1 : ROWS, :] * start_below
    )
    edge_g = compress(pad_rows(jnp.concatenate([edge_above, edge_below], axis=0), 8), block_w)
    local_g = part_g + edge_g[0:2]

    def event_copies(n, buf):
        return [
            pltpu.make_async_remote_copy(
                src_ref=buf.at[e],
                dst_ref=buf.at[e],
                send_sem=ev_send.at[n, k],
                recv_sem=ev_recv.at[n, k],
                device_id=((e + k) % EVENTS, t),
                device_id_type=MESH,
            )
            for k in range(1, EVENTS)
        ]

    ev1[e] = jnp.concatenate([local_w, local_g], axis=0)
    grad_copies = event_copies(0, ev1)
    for copy in grad_copies:
        copy.start()

    depth_o[...] = (scaled[...] + infilf[...] * (prolong(recharge) - scaled[...])).astype(BF16)

    for copy in head_copies:
        copy.wait()
    slot = iota((8, AROWS), 0)
    column = OWN * t + slot - jnp.where(slot < 6, 0, 8)
    known = jnp.where((column >= 0) & (column < ACOLS), 1.0, 0.0)
    offset = iota((LAYERS, 8, AROWS), 1)
    c_all = jnp.where((offset == 5) | (offset == 6), 0.0, cw[0:LAYERS]) * known[None]
    w_all = cw[LAYERS : 2 * LAYERS] * known[None]
    lk_all = cw[2 * LAYERS] * known
    blank = jnp.zeros((1, 8, AROWS), F32)

    def layered(field):
        return jnp.concatenate([field[1:], blank], axis=0) + jnp.concatenate(
            [blank, field[:-1]], axis=0
        )

    w_next = c_all * (neighbours4(w_all) + layered(w_all))
    base = (neighbours4(w_next) + layered(w_next))[:, 0:OWN, :]
    head_o[3:LAYERS] = base[3:LAYERS]

    all_of(1, ns, nr).wait()
    xs[...] = nr[...].T
    both = jnp.concatenate([xs[pl.ds(0, 8, stride=2), :], xs[pl.ds(1, 8, stride=2), :]], axis=1)
    leak = jnp.dot(pieces(both, 0), place_w[...], preferred_element_type=F32)
    leak = leak[0:8] + leak[8:16]
    ev2[e] = top_v[...] * leak[0:OWN]
    lk_copies = event_copies(1, ev2)
    for copy in lk_copies:
        copy.start()
    more_w = lk_all * leak
    next_zero = c_all[0] * neighbours4(more_w)
    next_one = c_all[1] * more_w
    charge_o[...] = (w_all[0] + w_next[0] + more_w + next_zero)[0:OWN]
    head_o[0] = base[0] + (neighbours4(next_zero) + next_one)[0:OWN]
    head_o[1] = base[1] + (next_zero + neighbours4(next_one))[0:OWN]
    head_o[2] = base[2] + next_one[0:OWN]

    for copy in grad_copies:
        copy.wait()
    total = ev1[0] + ev1[1] + ev1[2] + ev1[3]
    gw_o[...] = total[0:2]
    gg_o[...] = total[2:4]
    for copy in lk_copies:
        copy.wait()
    glk_o[...] = ev2[0] + ev2[1] + ev2[2] + ev2[3]


def hand_over(*refs):
    sem = refs[-1]
    half = len(refs) // 2
    copies = [
        pltpu.make_async_copy(source, target, sem.at[n])
        for n, (source, target) in enumerate(zip(refs[:half], refs[half:-1]))
    ]
    for copy in copies:
        copy.start()
    for copy in copies:
        copy.wait()


def per_device(
    surf_depth, surf_mid, surf_seed, stream, infil, diffus, leakance, active, jacobi_coef, head_seed, top_head
):
    args = (
        surf_seed[0], stream, diffus, jacobi_coef, active, leakance, head_seed[0], infil,
        surf_depth[0], surf_mid[0], top_head[0],
    )
    outs = [
        jax.ShapeDtypeStruct(shape, dtype)
        for shape, dtype in (
            ((ROWS, COLS), BF16),
            ((LAYERS, OWN, AROWS), F32),
            ((OWN, AROWS), F32),
            ((2, ACOLS), F32),
            ((2, ACOLS), F32),
            ((OWN, AROWS), F32),
        )
    ]
    vmem = pl.BlockSpec(memory_space=pltpu.VMEM)
    hbm = pl.BlockSpec(memory_space=pltpu.HBM)
    field = pltpu.VMEM((ROWS, COLS), F32)
    results = pl.pallas_call(
        step_kernel,
        out_shape=outs,
        in_specs=[hbm] * len(args),
        out_specs=[vmem] * len(outs),
        scratch_shapes=[pltpu.VMEM(a.shape, a.dtype) for a in args]
        + [field] * 7
        + [
            pltpu.VMEM((1024, 128), BF16),
            pltpu.VMEM((2, 1, COLS), F32),
            pltpu.VMEM((2, 1, COLS), F32),
            pltpu.VMEM((2, 2, COLS), F32),
            pltpu.VMEM((2, 2, COLS), F32),
            pltpu.VMEM((2, 2, COLS), F32),
            pltpu.VMEM((2, 2, COLS), F32),
            pltpu.VMEM((2, 2, ACOLS), F32),
            pltpu.VMEM((2, 2, ACOLS), F32),
            pltpu.VMEM((2 * LAYERS + 1, 8, AROWS), F32),
            pltpu.VMEM((128, 128), F32),
            pltpu.VMEM((TILES, 128), F32),
            pltpu.VMEM((TILES, 128), F32),
            pltpu.VMEM((TILES, 128), F32),
            pltpu.VMEM((TILES, 128), F32),
            pltpu.VMEM((EVENTS, 4, ACOLS), F32),
            pltpu.VMEM((EVENTS, OWN, AROWS), F32),
            pltpu.VMEM((TILES, 2 * ACOLS), BF16),
            pltpu.VMEM((256, AROWS), BF16),
            pltpu.SemaphoreType.DMA((len(args),)),
            pltpu.SemaphoreType.DMA((12,)),
            pltpu.SemaphoreType.DMA((12,)),
            pltpu.SemaphoreType.DMA((2,)),
            pltpu.SemaphoreType.DMA((2,)),
            pltpu.SemaphoreType.DMA((2, EVENTS)),
            pltpu.SemaphoreType.DMA((2, EVENTS)),
        ],
        compiler_params=pltpu.CompilerParams(
            collective_id=0, has_side_effects=True, vmem_limit_bytes=40 * 1024 * 1024
        ),
    )(*[pltpu.with_memory_space_constraint(a, pltpu.HBM) for a in args])
    depth, head, charge, grad_w, grad_g, grad_lk = pl.pallas_call(
        hand_over,
        out_shape=outs,
        in_specs=[pl.BlockSpec(memory_space=pl.ANY)] * len(outs),
        out_specs=[hbm] * len(outs),
        scratch_shapes=[pltpu.SemaphoreType.DMA((len(outs),))],
        compiler_params=pltpu.CompilerParams(vmem_limit_bytes=1024 * 1024),
    )(*results)
    return depth[None], head[None], charge[None], grad_w, grad_g, grad_lk


def solution(mesh):
    return jax.shard_map(
        per_device,
        mesh=mesh,
        in_specs=(
            P("event", "tile", None),
            P("event", "tile", None),
            P("event", "tile", None),
            P("tile", None),
            P("tile", None),
            P("tile", None),
            P("tile", None),
            P("tile", None),
            P(None, "tile", None),
            P("event", None, "tile", None),
            P("event", "tile", None),
        ),
        out_specs=(
            P("event", "tile", None),
            P("event", None, "tile", None),
            P("event", "tile", None),
            P("tile", None),
            P("tile", None),
            P("tile", None),
        ),
        check_vma=False,
    )
```
